32 devices in a mesh: grp: 1, seq: 16 (over z, y, core), prm: 2 (over x), hd: 1.
Axes of the slice: x: 2, y: 2, z: 4, core: 2. Of those that a mesh axis runs over, the one named last changes fastest.
Arguments:
- query_raw: bfloat16 [2, 2048, 16, 128], P(('grp', 'prm'), 'seq', 'hd'), may hold values from -6 to 6
- key_raw: bfloat16 [2, 2048, 2, 16, 128], P(('grp', 'prm'), 'seq', None, 'hd'), may hold values from -6 to 6
- value_raw: bfloat16 [2, 2048, 2, 16, 128], P(('grp', 'prm'), 'seq', None, 'hd'), may hold values from -110 to 110
- write_rate: float32 [2, 2048, 2, 16], P(('grp', 'prm'), 'seq', None, 'hd'), may hold values from 0 to 2
- decay_rate: float32 [2, 2048, 16], P(('grp', 'prm'), 'seq', 'hd'), may hold values from 0 to 1.5
- gate_input: bfloat16 [2, 2048, 16, 128], P(('grp', 'prm'), 'seq', 'hd'), may hold values from -6 to 6
- filter_query: float32 [4, 16, 128], P(None, 'hd'), may hold values from -4 to 4
- filter_key: float32 [4, 2, 16, 128], P(None, None, 'hd'), may hold values from -4 to 4
- filter_value: float32 [4, 2, 16, 128], P(None, None, 'hd'), may hold values from -4 to 4
- output_gain: float32 [16, 128], P('hd'), may hold values from 0.25 to 1.75
Outputs:
- mixed: bfloat16 [2, 2048, 16, 128], P(('grp', 'prm'), 'seq', 'hd')
The draws below stay inside these ranges and needn't reach their ends.
All inputs are finite; a program needn't handle non-finite values.
Results may differ from the reference program's by a relative error of at most 0.0012.
Values may be sent and summed in bfloat16 or wider, within the bound.
A program may use at most 128 MiB of HBM per device.

```python
import math
import jax
import jax.numpy as jnp
from jax import lax

HEAD_TOTAL = 16
DK = 128
DV = 128
REFL = 2
KW = 4
SPAN = 64
TOKEN_LENGTH = 2048
PROMPT_GROUP = 2


def head_speed(key):
    uniform_draw = jax.random.uniform(jax.random.fold_in(key, 101), (PROMPT_GROUP, 1, HEAD_TOTAL))
    fast_share = 0.5
    return jnp.where(uniform_draw < fast_share, 1.0, 0.0)


def draw_decay_rate(key, part):
    fast_heads = head_speed(key)
    fast_base = 1.0 / 40.0 * jnp.exp(jax.random.uniform(jax.random.fold_in(key, 1), (PROMPT_GROUP, 1, HEAD_TOTAL), minval=-0.3, maxval=0.3))
    slow_base = 0.15 / TOKEN_LENGTH
    baseline_speed = fast_heads * fast_base + (1.0 - fast_heads) * slow_base
    token_multiplier = jnp.exp(jax.random.uniform(jax.random.fold_in(key, 2), (PROMPT_GROUP, TOKEN_LENGTH, HEAD_TOTAL), minval=-0.7, maxval=0.7))
    block_multiplier = jnp.exp(jax.random.uniform(jax.random.fold_in(key, 3), (PROMPT_GROUP, TOKEN_LENGTH // SPAN, 1, HEAD_TOTAL), minval=-0.7, maxval=0.7))
    block_multiplier = jnp.repeat(block_multiplier, SPAN, axis=1).reshape(PROMPT_GROUP, TOKEN_LENGTH, HEAD_TOTAL)
    spike_locations = jax.random.randint(jax.random.fold_in(key, 4), (PROMPT_GROUP, 2, HEAD_TOTAL), 0, TOKEN_LENGTH)
    spike_penalty = jax.random.uniform(jax.random.fold_in(key, 5), (PROMPT_GROUP, 2, HEAD_TOTAL), minval=0.2, maxval=0.5)
    token_places = jnp.arange(TOKEN_LENGTH)[None, :, None, None]
    match_counts = jnp.where(token_places == spike_locations[:, None, :, :], 1.0, 0.0)
    spike_events = jnp.sum(match_counts * (-jnp.log(1.0 - spike_penalty))[:, None, :, :], axis=2)
    return (baseline_speed * token_multiplier * block_multiplier + spike_events).astype(jnp.float32)


def draw_write_rate(key, part):
    fast_heads = head_speed(key)[:, :, None, :]
    fast_value = jnp.exp(jax.random.uniform(jax.random.fold_in(key, 11), (PROMPT_GROUP, TOKEN_LENGTH, REFL, HEAD_TOTAL), minval=math.log(0.3), maxval=math.log(1.5)))
    slow_value = 0.15 * DK / TOKEN_LENGTH * jnp.exp(jax.random.uniform(jax.random.fold_in(key, 12), (PROMPT_GROUP, TOKEN_LENGTH, REFL, HEAD_TOTAL), minval=math.log(0.5), maxval=math.log(2.0)))
    mixed_value = fast_heads * fast_value + (1.0 - fast_heads) * slow_value
    return jnp.minimum(mixed_value, 1.9).astype(jnp.float32)


def draw_value_raw(key, part):
    shape_all = (PROMPT_GROUP, TOKEN_LENGTH, REFL, HEAD_TOTAL, DV)
    noise = jnp.clip(jax.random.normal(jax.random.fold_in(key, 23), shape_all), -4.0, 4.0)
    column_scale = jnp.exp(jax.random.uniform(jax.random.fold_in(key, 24), (1, 1, REFL, HEAD_TOTAL, DV), minval=0.0, maxval=math.log(10.0)))
    row_scale = jnp.exp(jax.random.uniform(jax.random.fold_in(key, 25), (PROMPT_GROUP, TOKEN_LENGTH, 1, 1, 1), minval=-1.0, maxval=1.0))
    return jnp.clip(noise * column_scale * row_scale, -110.0, 110.0).astype(jnp.bfloat16)


def block_levels(rng, dims, pieces, least, top_value):
    loudness, own = 1.0, jax.random.fold_in(rng, 6)
    for dim, parts in pieces:
        steps = jnp.exp(jax.random.uniform(jax.random.fold_in(own, dim), (parts,), jnp.float32, least / len(pieces), top_value / len(pieces)))
        loudness = loudness * jnp.repeat(steps, dims[dim] // parts).reshape([-1 if axis == dim else 1 for axis in range(len(dims))])
    return loudness


def bell_draw(rng, dims, scale, limit, cuts=(), kind=jnp.bfloat16):
    level = block_levels(rng, dims, cuts, -0.22, 0.18) if cuts else 1.0
    values = jax.random.normal(rng, dims, jnp.float32) * scale * level
    return jnp.minimum(jnp.maximum(values, -limit), limit).astype(kind)


def setup_inputs(seed: int = 0, part: int = 0) -> dict:
    splits = jax.random.split(jax.random.key(seed), 11)
    part_splits = jax.random.split(jax.random.fold_in(splits[10], part), 11)
    query_raw = bell_draw(part_splits[0], (PROMPT_GROUP, TOKEN_LENGTH, HEAD_TOTAL, DK), 1.0, 6.0, ((0, 2), (1, 16)))
    key_raw = bell_draw(part_splits[1], (PROMPT_GROUP, TOKEN_LENGTH, REFL, HEAD_TOTAL, DK), 1.0, 6.0, ((0, 2), (1, 16)))
    value_raw = draw_value_raw(jax.random.fold_in(jax.random.fold_in(splits[10], part), 71), part)
    write_rate = draw_write_rate(jax.random.fold_in(jax.random.fold_in(splits[10], part), 71), part)
    decay_rate = draw_decay_rate(jax.random.fold_in(jax.random.fold_in(splits[10], part), 71), part)
    gate_input = bell_draw(part_splits[5], (PROMPT_GROUP, TOKEN_LENGTH, HEAD_TOTAL, DV), 1.5, 6.0, ((0, 2), (1, 16)))
    filter_query = bell_draw(splits[6], (KW, HEAD_TOTAL, DK), 2 ** -0.5, 4.0, (), jnp.float32)
    filter_key = bell_draw(splits[7], (KW, REFL, HEAD_TOTAL, DK), 2 ** -0.5, 4.0, (), jnp.float32)
    filter_value = bell_draw(splits[8], (KW, REFL, HEAD_TOTAL, DV), 2 ** -0.5, 4.0, (), jnp.float32)
    output_gain = jnp.clip(1.0 + 0.15 * jax.random.normal(splits[9], (HEAD_TOTAL, DV), jnp.float32), 0.25, 1.75)
    return {"query_raw": query_raw, "key_raw": key_raw, "value_raw": value_raw, "write_rate": write_rate, "decay_rate": decay_rate, "gate_input": gate_input, "filter_query": filter_query, "filter_key": filter_key, "filter_value": filter_value, "output_gain": output_gain}


HIGH = lax.Precision.HIGHEST
epsilon = 1e-06

def short_conv(raw_input, kernel):
    tap_count = kernel.shape[0]
    tok_count = raw_input.shape[1]
    pad_widths = [(0, 0), (tap_count - 1, 0)] + [(0, 0)] * (raw_input.ndim - 2)
    padded = jnp.pad(raw_input.astype(jnp.float32), pad_widths)
    summed = jnp.zeros(raw_input.shape, jnp.float32)
    for tap_index in range(tap_count):
        summed = summed + kernel[tap_index] * padded[:, tap_index:tap_index + tok_count]
    return jax.nn.silu(summed)

def unit_norm(vectors):
    return vectors / jnp.sqrt(lax.optimization_barrier(jnp.sum(vectors * vectors, -1, keepdims=True)) + epsilon)

def reference(query_raw, key_raw, value_raw, write_rate, decay_rate, gate_input, filter_query, filter_key, filter_value, output_gain):
    queries = unit_norm(short_conv(query_raw, filter_query))
    keyset = unit_norm(short_conv(key_raw, filter_key))
    values = short_conv(value_raw, filter_value)

    def advance(carried, inputs_now):
        query_now, key_now, value_now, rate_now, decay_now = inputs_now
        carried = carried * jnp.exp(-decay_now)[:, :, None, None]
        for refl_index in range(key_now.shape[1]):
            key_one = key_now[:, refl_index]
            recalled = jnp.einsum('phk,phkv->phv', key_one, carried, precision=HIGH)
            update = (value_now[:, refl_index] - recalled)[:, :, None, :] * key_one[:, :, :, None]
            carried = carried + rate_now[:, refl_index][:, :, None, None] * update
        return (carried, jnp.einsum('phk,phkv->phv', query_now, carried, precision=HIGH))
    initial = jnp.zeros((queries.shape[0], queries.shape[2], keyset.shape[-1], values.shape[-1]), jnp.float32)
    final_state, outputs = lax.scan(advance, initial, (jnp.moveaxis(queries, 1, 0), jnp.moveaxis(keyset, 1, 0), jnp.moveaxis(values, 1, 0), jnp.moveaxis(write_rate, 1, 0), jnp.moveaxis(decay_rate, 1, 0)))
    outputs = jnp.moveaxis(outputs, 0, 1)
    normed = outputs / jnp.sqrt(lax.optimization_barrier(jnp.mean(outputs * outputs, -1, keepdims=True)) + epsilon)
    return (normed * output_gain * jax.nn.silu(gate_input.astype(jnp.float32))).astype(jnp.bfloat16)
```

```python
import functools

import jax
import jax.numpy as jnp
from jax import lax
from jax.experimental import pallas as pl
from jax.experimental.pallas import tpu as pltpu
from jax.sharding import PartitionSpec as P

HIGH = lax.Precision.HIGHEST
epsilon = 1e-06
CHUNK = 4
GROUP = 4
F32 = jnp.float32
BF16 = jnp.bfloat16


def split(x):
    hi = x.astype(BF16)
    return hi, (x - hi.astype(F32)).astype(BF16)


def dot(a, b):
    return jnp.dot(a, b, preferred_element_type=F32)


def dot_nt(a, b):
    return lax.dot_general(a, b, (((1,), (1,)), ((), ())), preferred_element_type=F32)


def pair(x):
    return jnp.concatenate(split(x), 1)


def mm_square(left_pair, right):
    rows = pair(right)
    out = dot(left_pair, jnp.concatenate([rows, rows], 0))
    width = right.shape[1]
    return out[:, :width] + out[:, width:]


def mm_wide(left, right):
    left_hi, left_lo = split(left)
    hi, lo = split(right)
    both = jnp.concatenate([left_hi, left_lo], 1)
    return dot(both, jnp.concatenate([hi, hi], 0)) + dot(left_hi, lo)


def mm_deep(left, right):
    left_hi, left_lo = split(left)
    hi, lo = split(right)
    return dot(left_hi, hi) + (dot(left_lo, hi) + dot(left_hi, lo))


def conv_into(x_ref, rim_ref, filter_ref, buf, normalize):
    taps = filter_ref.shape[0]
    rim = taps - 1
    tok = x_ref.shape[0]
    rows = CHUNK * (buf.shape[0] // tok)

    def finish(window, start):
        summed = jnp.zeros((CHUNK,) + window.shape[1:], F32)
        for tap in range(taps):
            summed = summed + filter_ref[tap] * window[tap : tap + CHUNK]
        out = jax.nn.silu(summed)
        if normalize:
            out = out / jnp.sqrt(jnp.sum(out * out, -1, keepdims=True) + epsilon)
        buf[pl.ds(start, rows), :] = out.reshape(rows, out.shape[-1])

    finish(
        jnp.concatenate([rim_ref[...].astype(F32), x_ref[0:CHUNK].astype(F32)], 0), 0
    )

    @pl.loop(1, tok // CHUNK)
    def _(step):
        window = x_ref[pl.ds(step * CHUNK - rim, CHUNK + rim)].astype(F32)
        finish(window, pl.multiple_of(step * rows, rows))


def local_kernel(
    q_ref, k_ref, v_ref, rq_ref, rk_ref, rv_ref, fq_ref, fk_ref, fv_ref,
    cum_ref, rate_ref, tok_ref, row_ref,
    pb_ref, ab_ref, q_buf, k_buf, v_buf,
):
    heads = q_ref.shape[1]
    tok = q_ref.shape[0]
    refl = k_ref.shape[1]
    steps = tok * refl
    group = pb_ref.shape[0]

    @pl.when(pl.program_id(0) == 0)
    def _():
        conv_into(q_ref, rq_ref, fq_ref, q_buf, True)
        conv_into(k_ref, rk_ref, fk_ref, k_buf, True)
        conv_into(v_ref, rv_ref, fv_ref, v_buf, False)

    half = steps // 2
    row = lax.broadcasted_iota(jnp.int32, (half, half), 0)
    col = lax.broadcasted_iota(jnp.int32, (half, half), 1)
    qrow = lax.broadcasted_iota(jnp.int32, (tok, steps), 0)
    qcol = lax.broadcasted_iota(jnp.int32, (tok, steps), 1)
    eye = jnp.where(row == col, 1.0, 0.0)
    dim = q_ref.shape[2]
    drow = lax.broadcasted_iota(jnp.int32, (dim, dim), 0)
    dcol = lax.broadcasted_iota(jnp.int32, (dim, dim), 1)

    work = []
    for g in range(group):
        head = pl.program_id(0) * group + g
        K = k_buf[pl.ds(head, steps, stride=heads), :]
        V = v_buf[pl.ds(head, steps, stride=heads), :]
        Q = q_buf[pl.ds(head, tok, stride=heads), :]
        cum = cum_ref[0, :, g : g + 1]
        rate = rate_ref[0, :, g : g + 1]
        cum_tok = tok_ref[0, :, g : g + 1]
        cum_row = row_ref[0, g : g + 1, :]
        last = cum_row[:, steps - 1 : steps]
        k_hi, k_lo = split(K)
        q_hi, q_lo = split(Q)
        hi = jnp.concatenate([k_hi, q_hi], 0)
        lo = jnp.concatenate([k_lo, q_lo], 0)
        gram = dot_nt(
            jnp.concatenate([hi, lo], 1), jnp.concatenate([k_hi, k_hi], 1)
        ) + dot_nt(hi, k_lo)

        def lower(r, c):
            ratio = jnp.exp(
                jnp.minimum(cum_row[:, c * half : (c + 1) * half] - cum[r * half : (r + 1) * half], 0.0)
            )
            block = gram[r * half : (r + 1) * half, c * half : (c + 1) * half]
            value = rate[r * half : (r + 1) * half] * ratio * block
            return jnp.where(row > col, value, 0.0) if r == c else value

        low = [lower(0, 0), lower(1, 1)]
        low_21 = lower(1, 0)
        mixing = jnp.where(
            qrow * refl + (refl - 1) >= qcol,
            gram[steps:] * jnp.exp(jnp.minimum(cum_row - cum_tok, 0.0)),
            0.0,
        )
        right = jnp.concatenate([(rate * jnp.exp(-cum)) * K, rate * V], 1)
        keys_t = K.T * jnp.exp(cum_row - last)
        work.append((low, low_21, mixing, right, keys_t, Q, cum_tok, last))

    inverse = [
        [eye - jnp.where((row // 2) == (col // 2), low, 0.0) for low in item[0]] for item in work
    ]
    size = 2
    while size < half:
        mask = ((row // (2 * size)) == (col // (2 * size))) & ((row // size) != (col // size))
        lefts = [[pair(x) for x in two] for two in inverse]
        inner = [
            [
                mm_square(pair(jnp.where(mask, low, 0.0)), x)
                for low, x in zip(item[0], two)
            ]
            for item, two in zip(work, inverse)
        ]
        inverse = [
            [x - mm_square(l, y) for x, l, y in zip(two, ls, ys)]
            for two, ls, ys in zip(inverse, lefts, inner)
        ]
        size *= 2

    for g, (item, two) in enumerate(zip(work, inverse)):
        low, low_21, mixing, right, keys_t, Q, cum_tok, last = item
        top = mm_wide(two[0], right[:half])
        bottom = mm_wide(two[1], right[half:] - mm_wide(low_21, top))
        solved = jnp.concatenate([top, bottom], 0)
        ab = mm_deep(keys_t, solved)
        pb = mm_deep(mixing, solved)
        ab_ref[g, :, :dim] = jnp.where(drow == dcol, jnp.exp(-last), 0.0) - ab[:, :dim]
        ab_ref[g, :, dim:] = ab[:, dim:]
        pb_ref[g, :, :dim] = jnp.exp(-cum_tok) * Q - pb[:, :dim]
        pb_ref[g, :, dim:] = pb[:, dim:]


def chain_kernel(ab_ref, s_ref, recv, send, send_sem, recv_sem):
    count = lax.axis_size("seq")
    me = lax.axis_index("seq")
    right = lax.rem(me + 1, count)
    left = lax.rem(me + count - 1, count)
    heads, dim = ab_ref.shape[0], ab_ref.shape[1]
    barrier = pltpu.get_barrier_semaphore()

    @pl.when(me > 0)
    def _():
        pl.semaphore_signal(
            barrier, inc=1, device_id={"seq": left}, device_id_type=pl.DeviceIdType.MESH
        )

    @pl.when(me < count - 1)
    def _():
        pl.semaphore_signal(
            barrier, inc=1, device_id={"seq": right}, device_id_type=pl.DeviceIdType.MESH
        )

    pl.semaphore_wait(barrier, jnp.minimum(me, 1) + jnp.minimum(count - 1 - me, 1))

    def copy(h):
        return pltpu.make_async_remote_copy(
            src_ref=send.at[h],
            dst_ref=recv.at[h],
            send_sem=send_sem.at[h],
            recv_sem=recv_sem.at[h],
            device_id={"seq": right},
            device_id_type=pl.DeviceIdType.MESH,
        )

    @pl.when(me == 0)
    def _():
        recv[...] = jnp.zeros_like(recv)

    @pl.loop(0, heads)
    def _(h):
        left_pair = pair(ab_ref[h, :, :dim])

        @pl.when(me > 0)
        def _():
            copy(h).wait_recv()

        state = recv[h]

        @pl.when(me < count - 1)
        def _():
            send[h] = mm_square(left_pair, state) + ab_ref[h, :, dim:]
            copy(h).start()

        s_ref[h] = state

    @pl.when(me < count - 1)
    def _():
        @pl.loop(0, heads)
        def _(h):
            copy(h).wait_send()


def out_kernel(pb_ref, s_ref, gate_ref, gain_ref, out_ref, buf):
    heads, tok, dim = pb_ref.shape[0], pb_ref.shape[1], pb_ref.shape[2] // 2

    @pl.loop(0, heads // GROUP)
    def _(step):
        for g in range(GROUP):
            h = step * GROUP + g
            value = mm_square(pair(pb_ref[h, :, :dim]), s_ref[h]) + pb_ref[h, :, dim:]
            buf[pl.ds(h, tok, stride=heads), :] = value

    rows = 8 * heads

    @pl.loop(0, tok // 8)
    def _(step):
        value = buf[pl.ds(pl.multiple_of(step * rows, rows), rows), :].reshape(8, heads, dim)
        normed = value / jnp.sqrt(jnp.mean(value * value, -1, keepdims=True) + epsilon)
        gate = jax.nn.silu(gate_ref[pl.ds(step * 8, 8)].astype(F32))
        out_ref[pl.ds(step * 8, 8)] = (normed * gain_ref[...] * gate).astype(out_ref.dtype)


VMEM = pl.BlockSpec(memory_space=pltpu.VMEM)


def one_prompt(q, k, v, rate, decay, gate, rims, fq, fk, fv, gain):
    tok, heads, dim = q.shape
    refl = k.shape[1]
    steps = tok * refl
    group = GROUP
    parts = heads // group
    order = lax.broadcasted_iota(jnp.int32, (tok, tok), 0) >= lax.broadcasted_iota(
        jnp.int32, (tok, tok), 1
    )
    cum = jnp.dot(order.astype(F32), decay, precision=HIGH)
    cum_steps = jnp.repeat(cum, refl, axis=0)

    def columns(x):
        return x.reshape(x.shape[0], parts, group).transpose(1, 0, 2)

    def whole(shape):
        return pl.BlockSpec(shape, lambda i: (0,) * len(shape))

    def part(shape):
        return pl.BlockSpec((1,) + shape, lambda i: (i, 0, 0))

    args = (
        q, k, v, rims[:, 0], rims[:, 1 : 1 + refl], rims[:, 1 + refl :], fq, fk, fv,
        columns(cum_steps), columns(rate.reshape(steps, heads)), columns(cum),
        cum_steps.T.reshape(parts, group, steps),
    )
    pb, ab = pl.pallas_call(
        local_kernel,
        grid=(parts,),
        in_specs=[whole(x.shape) for x in args[:9]]
        + [part((steps, group)), part((steps, group)), part((tok, group)), part((group, steps))],
        out_specs=[
            pl.BlockSpec((group, tok, 2 * dim), lambda i: (i, 0, 0)),
            pl.BlockSpec((group, dim, 2 * dim), lambda i: (i, 0, 0)),
        ],
        out_shape=[
            jax.ShapeDtypeStruct((heads, tok, 2 * dim), F32),
            jax.ShapeDtypeStruct((heads, dim, 2 * dim), F32),
        ],
        scratch_shapes=[
            pltpu.VMEM((tok * heads, dim), F32),
            pltpu.VMEM((steps * heads, dim), F32),
            pltpu.VMEM((steps * heads, dim), F32),
        ],
        compiler_params=pltpu.CompilerParams(vmem_limit_bytes=48 * 2**20),
    )(*args)
    states = pl.pallas_call(
        chain_kernel,
        in_specs=[VMEM],
        out_specs=VMEM,
        out_shape=jax.ShapeDtypeStruct((heads, dim, dim), F32),
        scratch_shapes=[
            pltpu.VMEM((heads, dim, dim), F32),
            pltpu.VMEM((heads, dim, dim), F32),
            pltpu.SemaphoreType.DMA((heads,)),
            pltpu.SemaphoreType.DMA((heads,)),
        ],
        compiler_params=pltpu.CompilerParams(
            collective_id=0, has_side_effects=True, vmem_limit_bytes=32 * 2**20
        ),
    )(ab)
    return pl.pallas_call(
        out_kernel,
        in_specs=[VMEM] * 4,
        out_specs=VMEM,
        out_shape=jax.ShapeDtypeStruct((tok, heads, dim), BF16),
        scratch_shapes=[pltpu.VMEM((tok * heads, dim), F32)],
        compiler_params=pltpu.CompilerParams(vmem_limit_bytes=32 * 2**20),
    )(pb, states, gate, gain)


def per_device(
    query_raw,
    key_raw,
    value_raw,
    write_rate,
    decay_rate,
    gate_input,
    filter_query,
    filter_key,
    filter_value,
    output_gain,
):
    rim_size = filter_query.shape[0] - 1
    start = query_raw.shape[1] - rim_size
    count = lax.axis_size("seq")
    edge = jnp.concatenate(
        [query_raw[:, start:, None], key_raw[:, start:], value_raw[:, start:]], 2
    )
    rims = lax.ppermute(edge, "seq", [(i, i + 1) for i in range(count - 1)])
    return jnp.stack(
        [
            one_prompt(
                query_raw[p], key_raw[p], value_raw[p], write_rate[p], decay_rate[p],
                gate_input[p], rims[p], filter_query, filter_key, filter_value, output_gain,
            )
            for p in range(query_raw.shape[0])
        ]
    )


def solution(mesh):
    return jax.shard_map(
        per_device,
        mesh=mesh,
        in_specs=(
            P(("grp", "prm"), "seq", "hd", None),
            P(("grp", "prm"), "seq", None, "hd", None),
            P(("grp", "prm"), "seq", None, "hd", None),
            P(("grp", "prm"), "seq", None, "hd"),
            P(("grp", "prm"), "seq", "hd"),
            P(("grp", "prm"), "seq", "hd", None),
            P(None, "hd", None),
            P(None, None, "hd", None),
            P(None, None, "hd", None),
            P("hd", None),
        ),
        out_specs=P(("grp", "prm"), "seq", "hd", None),
        check_vma=False,
    )
```

```python
import jax
import jax.numpy as jnp
from jax import lax
from jax.experimental import pallas as pl
from jax.experimental.pallas import tpu as pltpu
from jax.sharding import PartitionSpec as P

HIGH = lax.Precision.HIGHEST
epsilon = 1e-06
CHUNK = 4
GROUP = 4
F32 = jnp.float32
BF16 = jnp.bfloat16


def split(x):
    hi = x.astype(BF16)
    return hi, (x - hi.astype(F32)).astype(BF16)


def dot(a, b):
    return jnp.dot(a, b, preferred_element_type=F32)


def dot_nt(a, b):
    return lax.dot_general(a, b, (((1,), (1,)), ((), ())), preferred_element_type=F32)


def exact(a, b):
    return jnp.dot(a, b, precision=HIGH, preferred_element_type=F32)


def pair(x):
    return jnp.concatenate(split(x), 1)


def mm_square(left_pair, right):
    rows = pair(right)
    out = dot(left_pair, jnp.concatenate([rows, rows], 0))
    width = right.shape[1]
    return out[:, :width] + out[:, width:]


def mm_wide(left, right):
    left_hi, left_lo = split(left)
    hi, lo = split(right)
    both = jnp.concatenate([left_hi, left_lo], 1)
    return dot(both, jnp.concatenate([hi, hi], 0)) + dot(left_hi, lo)


def mm_deep(left, right):
    left_hi, left_lo = split(left)
    hi, lo = split(right)
    return dot(left_hi, hi) + (dot(left_lo, hi) + dot(left_hi, lo))


def conv_into(x_ref, rim_value, filter_ref, buf, normalize):
    taps = filter_ref.shape[0]
    rim = taps - 1
    tok = x_ref.shape[0]
    rows = CHUNK * (buf.shape[0] // tok)

    def finish(window, start):
        summed = jnp.zeros((CHUNK,) + window.shape[1:], F32)
        for tap in range(taps):
            summed = summed + filter_ref[tap] * window[tap : tap + CHUNK]
        out = jax.nn.silu(summed)
        if normalize:
            out = out / jnp.sqrt(jnp.sum(out * out, -1, keepdims=True) + epsilon)
        buf[pl.ds(start, rows), :] = out.reshape(rows, out.shape[-1])

    finish(
        jnp.concatenate([rim_value.astype(F32), x_ref[0:CHUNK].astype(F32)], 0), 0
    )

    @pl.loop(1, tok // CHUNK)
    def _(step):
        window = x_ref[pl.ds(step * CHUNK - rim, CHUNK + rim)].astype(F32)
        finish(window, pl.multiple_of(step * rows, rows))


def local_kernel(
    q_ref, k_ref, v_ref, rim_ref, fq_ref, fk_ref, fv_ref, decay_ref, rate_ref,
    pb_ref, ab_ref, q_buf, k_buf, v_buf, cum_buf, rate_buf, tok_buf,
):
    heads = q_ref.shape[1]
    tok = q_ref.shape[0]
    refl = k_ref.shape[1]
    steps = tok * refl
    group = pb_ref.shape[0]

    @pl.when(pl.program_id(0) == 0)
    def _():
        conv_into(q_ref, rim_ref[:, 0], fq_ref, q_buf, True)
        conv_into(k_ref, rim_ref[:, 1 : 1 + refl], fk_ref, k_buf, True)
        conv_into(v_ref, rim_ref[:, 1 + refl :], fv_ref, v_buf, False)
        step = lax.broadcasted_iota(jnp.int32, (steps, tok), 0)
        token = lax.broadcasted_iota(jnp.int32, (steps, tok), 1)
        decay = decay_ref[...]
        cum_buf[...] = exact(jnp.where(token * refl <= step, 1.0, 0.0), decay)
        trow = lax.broadcasted_iota(jnp.int32, (tok, tok), 0)
        tcol = lax.broadcasted_iota(jnp.int32, (tok, tok), 1)
        tok_buf[...] = exact(jnp.where(tcol <= trow, 1.0, 0.0), decay)
        rate_buf[...] = sum(
            exact(jnp.where(token * refl + j == step, 1.0, 0.0), rate_ref[:, j])
            for j in range(refl)
        )

    here = pl.program_id(0) * group
    pick = jnp.where(
        lax.broadcasted_iota(jnp.int32, (heads, 128), 0)
        == here + lax.broadcasted_iota(jnp.int32, (heads, 128), 1),
        1.0,
        0.0,
    )
    pick_rows = jnp.where(
        here + lax.broadcasted_iota(jnp.int32, (8, heads), 0)
        == lax.broadcasted_iota(jnp.int32, (8, heads), 1),
        1.0,
        0.0,
    )
    cums = exact(cum_buf[...], pick)
    rates = exact(rate_buf[...], pick)
    toks = exact(tok_buf[...], pick)
    cum_rows = lax.dot_general(
        pick_rows, cum_buf[...], (((1,), (1,)), ((), ())), precision=HIGH,
        preferred_element_type=F32,
    )

    half = steps // 2
    row = lax.broadcasted_iota(jnp.int32, (half, half), 0)
    col = lax.broadcasted_iota(jnp.int32, (half, half), 1)
    qrow = lax.broadcasted_iota(jnp.int32, (tok, steps), 0)
    qcol = lax.broadcasted_iota(jnp.int32, (tok, steps), 1)
    eye = jnp.where(row == col, 1.0, 0.0)
    dim = q_ref.shape[2]
    drow = lax.broadcasted_iota(jnp.int32, (dim, dim), 0)
    dcol = lax.broadcasted_iota(jnp.int32, (dim, dim), 1)

    work = []
    for g in range(group):
        head = pl.program_id(0) * group + g
        K = k_buf[pl.ds(head, steps, stride=heads), :]
        V = v_buf[pl.ds(head, steps, stride=heads), :]
        Q = q_buf[pl.ds(head, tok, stride=heads), :]
        cum = cums[:, g : g + 1]
        rate = rates[:, g : g + 1]
        cum_tok = toks[:, g : g + 1]
        cum_row = cum_rows[g : g + 1, :]
        last = cum_row[:, steps - 1 : steps]
        k_hi, k_lo = split(K)
        q_hi, q_lo = split(Q)
        hi = jnp.concatenate([k_hi, q_hi], 0)
        lo = jnp.concatenate([k_lo, q_lo], 0)
        gram = dot_nt(
            jnp.concatenate([hi, lo], 1), jnp.concatenate([k_hi, k_hi], 1)
        ) + dot_nt(hi, k_lo)

        def lower(r, c):
            ratio = jnp.exp(
                jnp.minimum(cum_row[:, c * half : (c + 1) * half] - cum[r * half : (r + 1) * half], 0.0)
            )
            block = gram[r * half : (r + 1) * half, c * half : (c + 1) * half]
            value = rate[r * half : (r + 1) * half] * ratio * block
            return jnp.where(row > col, value, 0.0) if r == c else value

        low = [lower(0, 0), lower(1, 1)]
        low_21 = lower(1, 0)
        mixing = jnp.where(
            qrow * refl + (refl - 1) >= qcol,
            gram[steps:] * jnp.exp(jnp.minimum(cum_row - cum_tok, 0.0)),
            0.0,
        )
        right = jnp.concatenate([(rate * jnp.exp(-cum)) * K, rate * V], 1)
        keys_t = K.T * jnp.exp(cum_row - last)
        work.append((low, low_21, mixing, right, keys_t, Q, cum_tok, last))

    inverse = [
        [eye - jnp.where((row // 2) == (col // 2), low, 0.0) for low in item[0]] for item in work
    ]
    size = 2
    while size < half:
        mask = ((row // (2 * size)) == (col // (2 * size))) & ((row // size) != (col // size))
        lefts = [[pair(x) for x in two] for two in inverse]
        inner = [
            [
                mm_square(pair(jnp.where(mask, low, 0.0)), x)
                for low, x in zip(item[0], two)
            ]
            for item, two in zip(work, inverse)
        ]
        inverse = [
            [x - mm_square(l, y) for x, l, y in zip(two, ls, ys)]
            for two, ls, ys in zip(inverse, lefts, inner)
        ]
        size *= 2

    for g, (item, two) in enumerate(zip(work, inverse)):
        low, low_21, mixing, right, keys_t, Q, cum_tok, last = item
        top = mm_wide(two[0], right[:half])
        bottom = mm_wide(two[1], right[half:] - mm_wide(low_21, top))
        solved = jnp.concatenate([top, bottom], 0)
        ab = mm_deep(keys_t, solved)
        pb = mm_deep(mixing, solved)
        ab_ref[g, :dim] = jnp.where(drow == dcol, jnp.exp(-last), 0.0) - ab[:, :dim].T
        ab_ref[g, dim:] = ab[:, dim:].T
        pb_ref[g, :, :dim] = jnp.exp(-cum_tok) * Q - pb[:, :dim]
        pb_ref[g, :, dim:] = pb[:, dim:]


def chain_kernel(
    ab_ref, s_ref, other, recv, send, back, mine,
    ex_send, ex_recv, st_send, st_recv, rt_send, rt_recv,
):
    count = lax.axis_size("seq")
    me = lax.axis_index("seq")
    side = lax.rem(me, 2)
    place = lax.div(me, 2)
    places = count // 2
    partner = me + 1 - 2 * side
    ahead = lax.rem(me + 2, count)
    behind = lax.rem(me + count - 2, count)
    heads, dim = ab_ref.shape[0], ab_ref.shape[2]
    half = heads // 2
    first = side * half
    barrier = pltpu.get_barrier_semaphore()

    def signal(device):
        pl.semaphore_signal(
            barrier, inc=1, device_id={"seq": device}, device_id_type=pl.DeviceIdType.MESH
        )

    signal(partner)

    @pl.when(place > 0)
    def _():
        signal(behind)

    @pl.when(place < places - 1)
    def _():
        signal(ahead)

    pl.semaphore_wait(
        barrier, 1 + jnp.minimum(place, 1) + jnp.minimum(places - 1 - place, 1)
    )

    def remote(src, dst, send_sem, recv_sem, device):
        return pltpu.make_async_remote_copy(
            src_ref=src, dst_ref=dst, send_sem=send_sem, recv_sem=recv_sem,
            device_id={"seq": device}, device_id_type=pl.DeviceIdType.MESH,
        )

    def exchange(i):
        return remote(
            ab_ref.at[half - first + i], other.at[i], ex_send.at[i], ex_recv.at[i], partner
        )

    def onward(i):
        return remote(send.at[i], recv.at[i], st_send.at[i], st_recv.at[i], ahead)

    def hand_back(i):
        return remote(back.at[i], mine.at[i], rt_send.at[i], rt_recv.at[i], partner)

    @pl.loop(0, half)
    def _(i):
        exchange(i).start()

    @pl.when(place == 0)
    def _():
        recv[...] = jnp.zeros_like(recv)

    @pl.loop(0, half)
    def _(i):
        exchange(i).wait_recv()
        own_map, other_map = ab_ref[first + i], other[i]
        early = jnp.where(side == 0, own_map, other_map)
        late = jnp.where(side == 0, other_map, own_map)
        joined = mm_square(pair(early), late[:dim])
        joined_b = joined[dim:] + late[dim:]

        @pl.when(place > 0)
        def _():
            onward(i).wait_recv()

        state = recv[i]
        state_pair = pair(state)

        @pl.when(place < places - 1)
        def _():
            send[i] = mm_square(state_pair, joined[:dim]) + joined_b
            onward(i).start()

        later = mm_square(state_pair, early[:dim]) + early[dim:]
        s_ref[first + i] = jnp.where(side == 0, state, later)
        back[i] = jnp.where(side == 0, later, state)
        hand_back(i).start()

    @pl.loop(0, half)
    def _(i):
        hand_back(i).wait_recv()
        s_ref[half - first + i] = mine[i]

    @pl.loop(0, half)
    def _(i):
        exchange(i).wait_send()
        hand_back(i).wait_send()

    @pl.when(place < places - 1)
    def _():
        @pl.loop(0, half)
        def _(i):
            onward(i).wait_send()


def out_kernel(pb_ref, s_ref, gate_ref, gain_ref, out_ref, buf):
    heads, tok, dim = pb_ref.shape[0], pb_ref.shape[1], pb_ref.shape[2] // 2

    @pl.loop(0, heads // GROUP)
    def _(step):
        for g in range(GROUP):
            h = step * GROUP + g
            value = mm_square(pair(pb_ref[h, :, :dim]), s_ref[h].T) + pb_ref[h, :, dim:]
            buf[pl.ds(h, tok, stride=heads), :] = value

    rows = 8 * heads

    @pl.loop(0, tok // 8)
    def _(step):
        value = buf[pl.ds(pl.multiple_of(step * rows, rows), rows), :].reshape(8, heads, dim)
        normed = value / jnp.sqrt(jnp.mean(value * value, -1, keepdims=True) + epsilon)
        gate = jax.nn.silu(gate_ref[pl.ds(step * 8, 8)].astype(F32))
        out_ref[pl.ds(step * 8, 8)] = (normed * gain_ref[...] * gate).astype(out_ref.dtype)


VMEM = pl.BlockSpec(memory_space=pltpu.VMEM)


def one_prompt(q, k, v, rate, decay, gate, rims, fq, fk, fv, gain):
    tok, heads, dim = q.shape
    refl = k.shape[1]
    steps = tok * refl
    group = GROUP
    parts = heads // group

    def whole(shape):
        return pl.BlockSpec(shape, lambda i: (0,) * len(shape))

    args = (q, k, v, rims, fq, fk, fv, decay, rate)
    pb, ab = pl.pallas_call(
        local_kernel,
        grid=(parts,),
        in_specs=[whole(x.shape) for x in args],
        out_specs=[
            pl.BlockSpec((group, tok, 2 * dim), lambda i: (i, 0, 0)),
            pl.BlockSpec((group, 2 * dim, dim), lambda i: (i, 0, 0)),
        ],
        out_shape=[
            jax.ShapeDtypeStruct((heads, tok, 2 * dim), F32),
            jax.ShapeDtypeStruct((heads, 2 * dim, dim), F32),
        ],
        scratch_shapes=[
            pltpu.VMEM((tok * heads, dim), F32),
            pltpu.VMEM((steps * heads, dim), F32),
            pltpu.VMEM((steps * heads, dim), F32),
            pltpu.VMEM((steps, heads), F32),
            pltpu.VMEM((steps, heads), F32),
            pltpu.VMEM((tok, heads), F32),
        ],
        compiler_params=pltpu.CompilerParams(vmem_limit_bytes=48 * 2**20),
    )(*args)
    states = pl.pallas_call(
        chain_kernel,
        in_specs=[VMEM],
        out_specs=VMEM,
        out_shape=jax.ShapeDtypeStruct((heads, dim, dim), F32),
        scratch_shapes=[
            pltpu.VMEM((heads // 2, 2 * dim, dim), F32),
        ]
        + [pltpu.VMEM((heads // 2, dim, dim), F32)] * 4
        + [pltpu.SemaphoreType.DMA((heads // 2,))] * 6,
        compiler_params=pltpu.CompilerParams(
            collective_id=0, has_side_effects=True, vmem_limit_bytes=32 * 2**20
        ),
    )(ab)
    return pl.pallas_call(
        out_kernel,
        in_specs=[VMEM] * 4,
        out_specs=VMEM,
        out_shape=jax.ShapeDtypeStruct((tok, heads, dim), BF16),
        scratch_shapes=[pltpu.VMEM((tok * heads, dim), F32)],
        compiler_params=pltpu.CompilerParams(vmem_limit_bytes=32 * 2**20),
    )(pb, states, gate, gain)


def per_device(
    query_raw,
    key_raw,
    value_raw,
    write_rate,
    decay_rate,
    gate_input,
    filter_query,
    filter_key,
    filter_value,
    output_gain,
):
    rim_size = filter_query.shape[0] - 1
    start = query_raw.shape[1] - rim_size
    count = lax.axis_size("seq")
    edge = jnp.concatenate(
        [query_raw[:, start:, None], key_raw[:, start:], value_raw[:, start:]], 2
    )
    rims = lax.ppermute(edge, "seq", [(i, i + 1) for i in range(count - 1)])
    return jnp.stack(
        [
            one_prompt(
                query_raw[p], key_raw[p], value_raw[p], write_rate[p], decay_rate[p],
                gate_input[p], rims[p], filter_query, filter_key, filter_value, output_gain,
            )
            for p in range(query_raw.shape[0])
        ]
    )


def solution(mesh):
    return jax.shard_map(
        per_device,
        mesh=mesh,
        in_specs=(
            P(("grp", "prm"), "seq", "hd", None),
            P(("grp", "prm"), "seq", None, "hd", None),
            P(("grp", "prm"), "seq", None, "hd", None),
            P(("grp", "prm"), "seq", None, "hd"),
            P(("grp", "prm"), "seq", "hd"),
            P(("grp", "prm"), "seq", "hd", None),
            P(None, "hd", None),
            P(None, None, "hd", None),
            P(None, None, "hd", None),
            P("hd", None),
        ),
        out_specs=P(("grp", "prm"), "seq", "hd", None),
        check_vma=False,
    )
```

```python
import jax
import jax.numpy as jnp
from jax import lax
from jax.experimental import pallas as pl
from jax.experimental.pallas import tpu as pltpu
from jax.sharding import PartitionSpec as P

HIGH = lax.Precision.HIGHEST
epsilon = 1e-06
CHUNK = 4
GROUP = 4
PIECES = 2
F32 = jnp.float32
BF16 = jnp.bfloat16


def split(x):
    hi = x.astype(BF16)
    return hi, (x - hi.astype(F32)).astype(BF16)


def dot(a, b):
    return jnp.dot(a, b, preferred_element_type=F32)


def dot_nt(a, b):
    return lax.dot_general(a, b, (((1,), (1,)), ((), ())), preferred_element_type=F32)


def exact(a, b):
    return jnp.dot(a, b, precision=HIGH, preferred_element_type=F32)


def pair(x):
    return jnp.concatenate(split(x), 1)


def mm_square(left_pair, right):
    rows = pair(right)
    out = dot(left_pair, jnp.concatenate([rows, rows], 0))
    width = right.shape[1]
    return out[:, :width] + out[:, width:]


def mm_wide(left, right):
    left_hi, left_lo = split(left)
    hi, lo = split(right)
    both = jnp.concatenate([left_hi, left_lo], 1)
    return dot(both, jnp.concatenate([hi, hi], 0)) + dot(left_hi, lo)


def mm_deep(left, right):
    left_hi, left_lo = split(left)
    hi, lo = split(right)
    return dot(left_hi, hi) + (dot(left_lo, hi) + dot(left_hi, lo))


def conv_into(x_ref, rim_ref, filter_ref, buf, normalize, edge):
    taps = filter_ref.shape[0]
    rim = taps - 1
    tok = x_ref.shape[0]
    rows = CHUNK * (buf.shape[0] // tok)

    def finish(window, start):
        summed = jnp.zeros((CHUNK,) + window.shape[1:], F32)
        for tap in range(taps):
            summed = summed + filter_ref[tap] * window[tap : tap + CHUNK]
        out = jax.nn.silu(summed)
        if normalize:
            out = out / jnp.sqrt(jnp.sum(out * out, -1, keepdims=True) + epsilon)
        buf[pl.ds(start, rows), :] = out.reshape(rows, out.shape[-1])

    if edge:
        finish(
            jnp.concatenate([rim_ref[...].astype(F32), x_ref[0:CHUNK].astype(F32)], 0), 0
        )
        return

    @pl.loop(1, tok // CHUNK)
    def _(step):
        window = x_ref[pl.ds(step * CHUNK - rim, CHUNK + rim)].astype(F32)
        finish(window, pl.multiple_of(step * rows, rows))


def shard_kernel(
    q_ref, k_ref, v_ref, fq_ref, fk_ref, fv_ref, decay_ref, rate_ref,
    pb_ref, s_ref,
    q_buf, k_buf, v_buf, cum_buf, rate_buf, tok_buf, rim_q, rim_k, rim_v,
    maps, other, recv, send, back, mine,
    rim_send, rim_recv, ex_send, ex_recv, st_send, st_recv, rt_send, rt_recv,
):
    heads, tok, refl, dim = q_ref.shape[1], q_ref.shape[0], k_ref.shape[1], q_ref.shape[2]
    steps = tok * refl
    group = pb_ref.shape[0]
    own = group // 2
    parts = heads // group
    rim = rim_q.shape[0]
    turn = pl.program_id(0)

    count = lax.axis_size("seq")
    me = lax.axis_index("seq")
    side = lax.rem(me, 2)
    place = lax.div(me, 2)
    places = count // 2
    partner = me + 1 - 2 * side
    first = side * own
    rest = own - first

    def remote(src, dst, send_sem, recv_sem, device):
        return pltpu.make_async_remote_copy(
            src_ref=src, dst_ref=dst, send_sem=send_sem, recv_sem=recv_sem,
            device_id={"seq": device}, device_id_type=pl.DeviceIdType.MESH,
        )

    def rim_copies():
        ends = ((q_ref, rim_q), (k_ref, rim_k), (v_ref, rim_v))
        return [
            remote(
                src.at[pl.ds(tok - rim, rim)], dst, rim_send.at[n], rim_recv.at[n],
                lax.rem(me + 1, count),
            )
            for n, (src, dst) in enumerate(ends)
        ]

    def exchange(g, j):
        slot = g * own + j
        return remote(
            maps.at[g * group + rest + j], other.at[slot],
            ex_send.at[slot], ex_recv.at[slot], partner,
        )

    def onward(g, j, piece):
        slot = (g * own + j) * PIECES + piece
        return remote(
            send.at[slot], recv.at[slot], st_send.at[slot], st_recv.at[slot],
            lax.rem(me + 2, count),
        )

    def hand_back(g, j):
        slot = g * own + j
        return remote(back.at[slot], mine.at[slot], rt_send.at[slot], rt_recv.at[slot], partner)

    @pl.when(turn == 0)
    def _():
        barrier = pltpu.get_barrier_semaphore()
        for shift in (-2, -1, 1, 2):

            @pl.when((me + shift >= 0) & (me + shift < count))
            def _():
                pl.semaphore_signal(
                    barrier, inc=1, device_id={"seq": lax.rem(me + shift + count, count)},
                    device_id_type=pl.DeviceIdType.MESH,
                )

        pl.semaphore_wait(barrier, jnp.minimum(me, 2) + jnp.minimum(count - 1 - me, 2))

        @pl.when(me < count - 1)
        def _():
            for one in rim_copies():
                one.start()

        @pl.when(me == 0)
        def _():
            for one in (rim_q, rim_k, rim_v):
                one[...] = jnp.zeros_like(one)

        @pl.when(place == 0)
        def _():
            recv[...] = jnp.zeros_like(recv)

        def convs(edge):
            conv_into(q_ref, rim_q, fq_ref, q_buf, True, edge)
            conv_into(k_ref, rim_k, fk_ref, k_buf, True, edge)
            conv_into(v_ref, rim_v, fv_ref, v_buf, False, edge)

        convs(False)
        step = lax.broadcasted_iota(jnp.int32, (steps, tok), 0)
        token = lax.broadcasted_iota(jnp.int32, (steps, tok), 1)
        decay = decay_ref[...]
        cum_buf[...] = exact(jnp.where(token * refl <= step, 1.0, 0.0), decay)
        trow = lax.broadcasted_iota(jnp.int32, (tok, tok), 0)
        tcol = lax.broadcasted_iota(jnp.int32, (tok, tok), 1)
        tok_buf[...] = exact(jnp.where(tcol <= trow, 1.0, 0.0), decay)
        rate_buf[...] = sum(
            exact(jnp.where(token * refl + j == step, 1.0, 0.0), rate_ref[:, j])
            for j in range(refl)
        )

        @pl.when(me > 0)
        def _():
            for one in rim_copies():
                one.wait_recv()

        convs(True)

        @pl.when(me < count - 1)
        def _():
            for one in rim_copies():
                one.wait_send()

    @pl.when(turn < parts)
    def _():
        here = turn * group
        pick = jnp.where(
            lax.broadcasted_iota(jnp.int32, (heads, 128), 0)
            == here + lax.broadcasted_iota(jnp.int32, (heads, 128), 1),
            1.0,
            0.0,
        )
        pick_rows = jnp.where(
            here + lax.broadcasted_iota(jnp.int32, (8, heads), 0)
            == lax.broadcasted_iota(jnp.int32, (8, heads), 1),
            1.0,
            0.0,
        )
        cums = exact(cum_buf[...], pick)
        rates = exact(rate_buf[...], pick)
        toks = exact(tok_buf[...], pick)
        cum_rows = lax.dot_general(
            pick_rows, cum_buf[...], (((1,), (1,)), ((), ())), precision=HIGH,
            preferred_element_type=F32,
        )

        half = steps // 2
        row = lax.broadcasted_iota(jnp.int32, (half, half), 0)
        col = lax.broadcasted_iota(jnp.int32, (half, half), 1)
        qrow = lax.broadcasted_iota(jnp.int32, (tok, steps), 0)
        qcol = lax.broadcasted_iota(jnp.int32, (tok, steps), 1)
        eye = jnp.where(row == col, 1.0, 0.0)
        dim = q_ref.shape[2]
        drow = lax.broadcasted_iota(jnp.int32, (dim, dim), 0)
        dcol = lax.broadcasted_iota(jnp.int32, (dim, dim), 1)

        work = []
        for g in range(group):
            head = here + g
            K = k_buf[pl.ds(head, steps, stride=heads), :]
            V = v_buf[pl.ds(head, steps, stride=heads), :]
            Q = q_buf[pl.ds(head, tok, stride=heads), :]
            cum = cums[:, g : g + 1]
            rate = rates[:, g : g + 1]
            cum_tok = toks[:, g : g + 1]
            cum_row = cum_rows[g : g + 1, :]
            last = cum_row[:, steps - 1 : steps]
            k_hi, k_lo = split(K)
            q_hi, q_lo = split(Q)
            hi = jnp.concatenate([k_hi, q_hi], 0)
            lo = jnp.concatenate([k_lo, q_lo], 0)
            gram = dot_nt(
                jnp.concatenate([hi, lo], 1), jnp.concatenate([k_hi, k_hi], 1)
            ) + dot_nt(hi, k_lo)

            def lower(r, c):
                ratio = jnp.exp(
                    jnp.minimum(cum_row[:, c * half : (c + 1) * half] - cum[r * half : (r + 1) * half], 0.0)
                )
                block = gram[r * half : (r + 1) * half, c * half : (c + 1) * half]
                value = rate[r * half : (r + 1) * half] * ratio * block
                return jnp.where(row > col, value, 0.0) if r == c else value

            low = [lower(0, 0), lower(1, 1)]
            low_21 = lower(1, 0)
            mixing = jnp.where(
                qrow * refl + (refl - 1) >= qcol,
                gram[steps:] * jnp.exp(jnp.minimum(cum_row - cum_tok, 0.0)),
                0.0,
            )
            right = jnp.concatenate([(rate * jnp.exp(-cum)) * K, rate * V], 1)
            keys_t = K.T * jnp.exp(cum_row - last)
            work.append((low, low_21, mixing, right, keys_t, Q, cum_tok, last))

        inverse = [
            [eye - jnp.where((row // 2) == (col // 2), low, 0.0) for low in item[0]] for item in work
        ]
        size = 2
        while size < half:
            mask = ((row // (2 * size)) == (col // (2 * size))) & ((row // size) != (col // size))
            lefts = [[pair(x) for x in two] for two in inverse]
            inner = [
                [
                    mm_square(pair(jnp.where(mask, low, 0.0)), x)
                    for low, x in zip(item[0], two)
                ]
                for item, two in zip(work, inverse)
            ]
            inverse = [
                [x - mm_square(l, y) for x, l, y in zip(two, ls, ys)]
                for two, ls, ys in zip(inverse, lefts, inner)
            ]
            size *= 2

        for g, (item, two) in enumerate(zip(work, inverse)):
            low, low_21, mixing, right, keys_t, Q, cum_tok, last = item
            top = mm_wide(two[0], right[:half])
            bottom = mm_wide(two[1], right[half:] - mm_wide(low_21, top))
            solved = jnp.concatenate([top, bottom], 0)
            ab = mm_deep(keys_t, solved)
            pb = mm_deep(mixing, solved)
            maps[here + g, :dim] = jnp.where(drow == dcol, jnp.exp(-last), 0.0) - ab[:, :dim].T
            maps[here + g, dim:] = ab[:, dim:].T
            pb_ref[g, :, :dim] = jnp.exp(-cum_tok) * Q - pb[:, :dim]
            pb_ref[g, :, dim:] = pb[:, dim:]

        for j in range(own):
            exchange(turn, j).start()

    @pl.when(turn > 0)
    def _():
        g = turn - 1
        joins = []
        for j in range(own):
            exchange(g, j).wait_recv()
            own_map, other_map = maps[g * group + first + j], other[g * own + j]
            early = jnp.where(side == 0, own_map, other_map)
            late = jnp.where(side == 0, other_map, own_map)
            joined = mm_square(pair(early), late[:dim])
            joins.append((joined[:dim], joined[dim:] + late[dim:], early))
        rows = dim // PIECES
        for j in range(own):
            for piece in range(PIECES):

                @pl.when(place > 0)
                def _():
                    onward(g, j, piece).wait_recv()

                slot = (g * own + j) * PIECES + piece
                state_pair = pair(recv[slot])
                send[slot] = mm_square(state_pair, joins[j][0]) + joins[j][1][
                    piece * rows : (piece + 1) * rows
                ]

                @pl.when(place < places - 1)
                def _():
                    onward(g, j, piece).start()

        for j in range(own):
            slot = g * own + j
            state = jnp.concatenate([recv[slot * PIECES + piece] for piece in range(PIECES)], 0)
            early = joins[j][2]
            later = mm_square(pair(state), early[:dim]) + early[dim:]
            s_ref[g * group + first + j] = jnp.where(side == 0, state, later)
            back[slot] = jnp.where(side == 0, later, state)
            hand_back(g, j).start()

    @pl.when(turn == parts)
    def _():
        @pl.loop(0, parts)
        def _(g):
            for j in range(own):
                hand_back(g, j).wait_recv()
                s_ref[g * group + rest + j] = mine[g * own + j]
                exchange(g, j).wait_send()
                hand_back(g, j).wait_send()

        @pl.when(place < places - 1)
        def _():
            @pl.loop(0, parts)
            def _(g):
                for j in range(own):
                    for piece in range(PIECES):
                        onward(g, j, piece).wait_send()


def out_kernel(pb_ref, s_ref, gate_ref, gain_ref, out_ref, buf):
    heads, tok, dim = pb_ref.shape[0], pb_ref.shape[1], pb_ref.shape[2] // 2

    @pl.loop(0, heads // GROUP)
    def _(step):
        for g in range(GROUP):
            h = step * GROUP + g
            value = mm_square(pair(pb_ref[h, :, :dim]), s_ref[h].T) + pb_ref[h, :, dim:]
            buf[pl.ds(h, tok, stride=heads), :] = value

    rows = 8 * heads

    @pl.loop(0, tok // 8)
    def _(step):
        value = buf[pl.ds(pl.multiple_of(step * rows, rows), rows), :].reshape(8, heads, dim)
        normed = value / jnp.sqrt(jnp.mean(value * value, -1, keepdims=True) + epsilon)
        gate = jax.nn.silu(gate_ref[pl.ds(step * 8, 8)].astype(F32))
        out_ref[pl.ds(step * 8, 8)] = (normed * gain_ref[...] * gate).astype(out_ref.dtype)


VMEM = pl.BlockSpec(memory_space=pltpu.VMEM)


def one_prompt(q, k, v, rate, decay, gate, fq, fk, fv, gain):
    tok, heads, dim = q.shape
    refl = k.shape[1]
    steps = tok * refl
    group = GROUP
    parts = heads // group

    def whole(shape):
        return pl.BlockSpec(shape, lambda i: (0,) * len(shape))

    args = (q, k, v, fq, fk, fv, decay, rate)
    half = heads // 2
    rim = fq.shape[0] - 1
    dma = pltpu.SemaphoreType.DMA
    pb, states = pl.pallas_call(
        shard_kernel,
        grid=(parts + 1,),
        in_specs=[whole(x.shape) for x in args],
        out_specs=[
            pl.BlockSpec(
                (group, tok, 2 * dim), lambda i: (jnp.minimum(i, parts - 1), 0, 0)
            ),
            whole((heads, dim, dim)),
        ],
        out_shape=[
            jax.ShapeDtypeStruct((heads, tok, 2 * dim), F32),
            jax.ShapeDtypeStruct((heads, dim, dim), F32),
        ],
        scratch_shapes=[
            pltpu.VMEM((tok * heads, dim), F32),
            pltpu.VMEM((steps * heads, dim), F32),
            pltpu.VMEM((steps * heads, dim), F32),
            pltpu.VMEM((steps, heads), F32),
            pltpu.VMEM((steps, heads), F32),
            pltpu.VMEM((tok, heads), F32),
            pltpu.VMEM((rim, heads, dim), BF16),
            pltpu.VMEM((rim, refl, heads, dim), BF16),
            pltpu.VMEM((rim, refl, heads, dim), BF16),
            pltpu.VMEM((heads, 2 * dim, dim), F32),
            pltpu.VMEM((half, 2 * dim, dim), F32),
            pltpu.VMEM((half * PIECES, dim // PIECES, dim), F32),
            pltpu.VMEM((half * PIECES, dim // PIECES, dim), F32),
            pltpu.VMEM((half, dim, dim), F32),
            pltpu.VMEM((half, dim, dim), F32),
            dma((3,)), dma((3,)), dma((half,)), dma((half,)),
            dma((half * PIECES,)), dma((half * PIECES,)), dma((half,)), dma((half,)),
        ],
        compiler_params=pltpu.CompilerParams(
            collective_id=0, has_side_effects=True, vmem_limit_bytes=58 * 2**20
        ),
    )(*args)
    return pl.pallas_call(
        out_kernel,
        in_specs=[VMEM] * 4,
        out_specs=VMEM,
        out_shape=jax.ShapeDtypeStruct((tok, heads, dim), BF16),
        scratch_shapes=[pltpu.VMEM((tok * heads, dim), F32)],
        compiler_params=pltpu.CompilerParams(vmem_limit_bytes=32 * 2**20),
    )(pb, states, gate, gain)


def per_device(
    query_raw,
    key_raw,
    value_raw,
    write_rate,
    decay_rate,
    gate_input,
    filter_query,
    filter_key,
    filter_value,
    output_gain,
):
    return jnp.stack(
        [
            one_prompt(
                query_raw[p], key_raw[p], value_raw[p], write_rate[p], decay_rate[p],
                gate_input[p], filter_query, filter_key, filter_value, output_gain,
            )
            for p in range(query_raw.shape[0])
        ]
    )


def solution(mesh):
    return jax.shard_map(
        per_device,
        mesh=mesh,
        in_specs=(
            P(("grp", "prm"), "seq", "hd", None),
            P(("grp", "prm"), "seq", None, "hd", None),
            P(("grp", "prm"), "seq", None, "hd", None),
            P(("grp", "prm"), "seq", None, "hd"),
            P(("grp", "prm"), "seq", "hd"),
            P(("grp", "prm"), "seq", "hd", None),
            P(None, "hd", None),
            P(None, None, "hd", None),
            P(None, None, "hd", None),
            P("hd", None),
        ),
        out_specs=P(("grp", "prm"), "seq", "hd", None),
        check_vma=False,
    )
```

```python
import jax
import jax.numpy as jnp
from jax import lax
from jax.experimental import pallas as pl
from jax.experimental.pallas import tpu as pltpu
from jax.sharding import PartitionSpec as P

HIGH = lax.Precision.HIGHEST
epsilon = 1e-06
CHUNK = 4
GROUP = 4
PIECES = 2
SHARE = 4
F32 = jnp.float32
BF16 = jnp.bfloat16


def split(x):
    hi = x.astype(BF16)
    return hi, (x - hi.astype(F32)).astype(BF16)


def dot(a, b):
    return jnp.dot(a, b, preferred_element_type=F32)


def dot_nt(a, b):
    return lax.dot_general(a, b, (((1,), (1,)), ((), ())), preferred_element_type=F32)


def exact(a, b):
    return jnp.dot(a, b, precision=HIGH, preferred_element_type=F32)


def exact_nt(a, b):
    return lax.dot_general(
        a, b, (((1,), (1,)), ((), ())), precision=HIGH, preferred_element_type=F32
    )


def pair(x):
    return jnp.concatenate(split(x), 1)


def mm_square(left_pair, right):
    rows = pair(right)
    out = dot(left_pair, jnp.concatenate([rows, rows], 0))
    width = right.shape[1]
    return out[:, :width] + out[:, width:]


def mm_wide(left, right):
    left_hi, left_lo = split(left)
    hi, lo = split(right)
    both = jnp.concatenate([left_hi, left_lo], 1)
    return dot(both, jnp.concatenate([hi, hi], 0)) + dot(left_hi, lo)


def mm_deep(left, right):
    left_hi, left_lo = split(left)
    hi, lo = split(right)
    return dot(left_hi, hi) + (dot(left_lo, hi) + dot(left_hi, lo))


def conv_into(x_ref, rim_ref, filter_ref, buf, normalize, edge):
    taps = filter_ref.shape[0]
    rim = taps - 1
    tok = x_ref.shape[0]
    rows = CHUNK * (buf.shape[0] // tok)

    def finish(window, start):
        summed = jnp.zeros((CHUNK,) + window.shape[1:], F32)
        for tap in range(taps):
            summed = summed + filter_ref[tap] * window[tap : tap + CHUNK]
        out = jax.nn.silu(summed)
        if normalize:
            out = out / jnp.sqrt(jnp.sum(out * out, -1, keepdims=True) + epsilon)
        buf[pl.ds(start, rows), :] = out.reshape(rows, out.shape[-1])

    if edge:
        finish(
            jnp.concatenate([rim_ref[...].astype(F32), x_ref[0:CHUNK].astype(F32)], 0), 0
        )
        return

    @pl.loop(1, tok // CHUNK)
    def _(step):
        window = x_ref[pl.ds(step * CHUNK - rim, CHUNK + rim)].astype(F32)
        finish(window, pl.multiple_of(step * rows, rows))


def shard_kernel(
    q_ref, k_ref, v_ref, fq_ref, fk_ref, fv_ref, decay_ref, rate_ref,
    pb_ref, s_ref,
    q_buf, k_buf, v_buf, cum_buf, rate_buf, tok_buf, rim_q, rim_k, rim_v,
    maps, other, recv, send, back, mine,
    rim_send, rim_recv, ex_send, ex_recv, st_send, st_recv, rt_send, rt_recv,
):
    heads, tok, refl, dim = q_ref.shape[1], q_ref.shape[0], k_ref.shape[1], q_ref.shape[2]
    steps = tok * refl
    group = pb_ref.shape[0]
    own = group // SHARE
    parts = heads // group
    rim = rim_q.shape[0]
    turn = pl.program_id(0)

    count = lax.axis_size("seq")
    me = lax.axis_index("seq")
    side = lax.rem(me, SHARE)
    place = lax.div(me, SHARE)
    places = count // SHARE
    base = place * SHARE
    first = side * own

    def remote(src, dst, send_sem, recv_sem, device):
        return pltpu.make_async_remote_copy(
            src_ref=src, dst_ref=dst, send_sem=send_sem, recv_sem=recv_sem,
            device_id={"seq": device}, device_id_type=pl.DeviceIdType.MESH,
        )

    def rim_copies():
        ends = ((q_ref, rim_q), (k_ref, rim_k), (v_ref, rim_v))
        return [
            remote(
                src.at[pl.ds(tok - rim, rim)], dst, rim_send.at[n], rim_recv.at[n],
                lax.rem(me + 1, count),
            )
            for n, (src, dst) in enumerate(ends)
        ]

    def peer_side(d):
        return lax.rem(side + d, SHARE)

    def exchange(g, j, d, arriving=False):
        slot = g * own + j
        peer = peer_side(d)
        source = peer if arriving else side
        return remote(
            maps.at[g * group + peer * own + j], other.at[slot * SHARE + source],
            ex_send.at[slot * SHARE + d], ex_recv.at[slot * SHARE + source], base + peer,
        )

    def onward(g, j, piece):
        slot = (g * own + j) * PIECES + piece
        return remote(
            send.at[slot], recv.at[slot], st_send.at[slot], st_recv.at[slot],
            lax.rem(me + SHARE, count),
        )

    def hand_back(g, j, d, arriving=False):
        slot = g * own + j
        peer = peer_side(d)
        head = g * group + (peer if arriving else side) * own + j
        return remote(
            back.at[slot * SHARE + peer], mine.at[head],
            rt_send.at[slot * SHARE + d], rt_recv.at[head], base + peer,
        )

    @pl.when(turn == 0)
    def _():
        barrier = pltpu.get_barrier_semaphore()

        def signal(device):
            pl.semaphore_signal(
                barrier, inc=1, device_id={"seq": lax.rem(device + count, count)},
                device_id_type=pl.DeviceIdType.MESH,
            )

        for d in range(1, SHARE):
            signal(base + peer_side(d))

        @pl.when(place > 0)
        def _():
            signal(me - SHARE)

            @pl.when(side == 0)
            def _():
                signal(me - 1)

        @pl.when(place < places - 1)
        def _():
            signal(me + SHARE)

            @pl.when(side == SHARE - 1)
            def _():
                signal(me + 1)

        before, after = jnp.minimum(place, 1), jnp.minimum(places - 1 - place, 1)
        peers = SHARE - 1 + before + after
        peers += before * (1 - jnp.minimum(side, 1))
        peers += after * (1 - jnp.minimum(SHARE - 1 - side, 1))
        pl.semaphore_wait(barrier, peers)

        @pl.when(me < count - 1)
        def _():
            for one in rim_copies():
                one.start()

        @pl.when(me == 0)
        def _():
            for one in (rim_q, rim_k, rim_v):
                one[...] = jnp.zeros_like(one)

        @pl.when(place == 0)
        def _():
            recv[...] = jnp.zeros_like(recv)

        def convs(edge):
            conv_into(q_ref, rim_q, fq_ref, q_buf, True, edge)
            conv_into(k_ref, rim_k, fk_ref, k_buf, True, edge)
            conv_into(v_ref, rim_v, fv_ref, v_buf, False, edge)

        convs(False)
        step = lax.broadcasted_iota(jnp.int32, (steps, tok), 0)
        token = lax.broadcasted_iota(jnp.int32, (steps, tok), 1)
        decay = decay_ref[...]
        cum_buf[...] = exact_nt(jnp.where(token * refl <= step, 1.0, 0.0), decay)
        trow = lax.broadcasted_iota(jnp.int32, (tok, tok), 0)
        tcol = lax.broadcasted_iota(jnp.int32, (tok, tok), 1)
        tok_buf[...] = exact_nt(jnp.where(tcol <= trow, 1.0, 0.0), decay)
        rate_buf[...] = sum(
            exact_nt(jnp.where(token * refl + j == step, 1.0, 0.0), rate_ref[j])
            for j in range(refl)
        )

        @pl.when(me > 0)
        def _():
            for one in rim_copies():
                one.wait_recv()

        convs(True)

        @pl.when(me < count - 1)
        def _():
            for one in rim_copies():
                one.wait_send()

    @pl.when(turn < parts)
    def _():
        here = turn * group
        pick = jnp.where(
            lax.broadcasted_iota(jnp.int32, (heads, 128), 0)
            == here + lax.broadcasted_iota(jnp.int32, (heads, 128), 1),
            1.0,
            0.0,
        )
        pick_rows = jnp.where(
            here + lax.broadcasted_iota(jnp.int32, (8, heads), 0)
            == lax.broadcasted_iota(jnp.int32, (8, heads), 1),
            1.0,
            0.0,
        )
        cums = exact(cum_buf[...], pick)
        rates = exact(rate_buf[...], pick)
        toks = exact(tok_buf[...], pick)
        cum_rows = lax.dot_general(
            pick_rows, cum_buf[...], (((1,), (1,)), ((), ())), precision=HIGH,
            preferred_element_type=F32,
        )

        half = steps // 2
        row = lax.broadcasted_iota(jnp.int32, (half, half), 0)
        col = lax.broadcasted_iota(jnp.int32, (half, half), 1)
        qrow = lax.broadcasted_iota(jnp.int32, (tok, steps), 0)
        qcol = lax.broadcasted_iota(jnp.int32, (tok, steps), 1)
        eye = jnp.where(row == col, 1.0, 0.0)
        dim = q_ref.shape[2]
        drow = lax.broadcasted_iota(jnp.int32, (dim, dim), 0)
        dcol = lax.broadcasted_iota(jnp.int32, (dim, dim), 1)

        work = []
        for g in range(group):
            head = here + g
            K = k_buf[pl.ds(head, steps, stride=heads), :]
            V = v_buf[pl.ds(head, steps, stride=heads), :]
            Q = q_buf[pl.ds(head, tok, stride=heads), :]
            cum = cums[:, g : g + 1]
            rate = rates[:, g : g + 1]
            cum_tok = toks[:, g : g + 1]
            cum_row = cum_rows[g : g + 1, :]
            last = cum_row[:, steps - 1 : steps]
            k_hi, k_lo = split(K)
            q_hi, q_lo = split(Q)
            hi = jnp.concatenate([k_hi, q_hi], 0)
            lo = jnp.concatenate([k_lo, q_lo], 0)
            gram = dot_nt(
                jnp.concatenate([hi, lo], 1), jnp.concatenate([k_hi, k_hi], 1)
            ) + dot_nt(hi, k_lo)

            def lower(r, c):
                ratio = jnp.exp(
                    jnp.minimum(cum_row[:, c * half : (c + 1) * half] - cum[r * half : (r + 1) * half], 0.0)
                )
                block = gram[r * half : (r + 1) * half, c * half : (c + 1) * half]
                value = rate[r * half : (r + 1) * half] * ratio * block
                return jnp.where(row > col, value, 0.0) if r == c else value

            low = [lower(0, 0), lower(1, 1)]
            low_21 = lower(1, 0)
            mixing = jnp.where(
                qrow * refl + (refl - 1) >= qcol,
                gram[steps:] * jnp.exp(jnp.minimum(cum_row - cum_tok, 0.0)),
                0.0,
            )
            right = jnp.concatenate([(rate * jnp.exp(-cum)) * K, rate * V], 1)
            keys_t = K.T * jnp.exp(cum_row - last)
            work.append((low, low_21, mixing, right, keys_t, Q, cum_tok, last))

        inverse = [
            [eye - jnp.where((row // 2) == (col // 2), low, 0.0) for low in item[0]] for item in work
        ]
        size = 2
        while size < half:
            mask = ((row // (2 * size)) == (col // (2 * size))) & ((row // size) != (col // size))
            lefts = [[pair(x) for x in two] for two in inverse]
            inner = [
                [
                    mm_square(pair(jnp.where(mask, low, 0.0)), x)
                    for low, x in zip(item[0], two)
                ]
                for item, two in zip(work, inverse)
            ]
            inverse = [
                [x - mm_square(l, y) for x, l, y in zip(two, ls, ys)]
                for two, ls, ys in zip(inverse, lefts, inner)
            ]
            size *= 2

        for g, (item, two) in enumerate(zip(work, inverse)):
            low, low_21, mixing, right, keys_t, Q, cum_tok, last = item
            top = mm_wide(two[0], right[:half])
            bottom = mm_wide(two[1], right[half:] - mm_wide(low_21, top))
            solved = jnp.concatenate([top, bottom], 0)
            ab = mm_deep(keys_t, solved)
            pb = mm_deep(mixing, solved)
            maps[here + g, :dim] = jnp.where(drow == dcol, jnp.exp(-last), 0.0) - ab[:, :dim].T
            maps[here + g, dim:] = ab[:, dim:].T
            pb_ref[g, :, :dim] = jnp.exp(-cum_tok) * Q - pb[:, :dim]
            pb_ref[g, :, dim:] = pb[:, dim:]

        for j in range(own):
            for d in range(1, SHARE):
                exchange(turn, j, d).start()
            other[(turn * own + j) * SHARE + side] = maps[here + first + j]

    @pl.when(turn > 0)
    def _():
        g = turn - 1
        joins = []
        for j in range(own):
            for d in range(1, SHARE):
                exchange(g, j, d, True).wait_recv()
            joined = other[(g * own + j) * SHARE]
            for n in range(1, SHARE):
                late = other[(g * own + j) * SHARE + n]
                product = mm_square(pair(joined), late[:dim])
                joined = jnp.concatenate([product[:dim], product[dim:] + late[dim:]], 0)
            joins.append((joined[:dim], joined[dim:]))
        rows = dim // PIECES
        for j in range(own):
            for piece in range(PIECES):

                @pl.when(place > 0)
                def _():
                    onward(g, j, piece).wait_recv()

                slot = (g * own + j) * PIECES + piece
                state_pair = pair(recv[slot])
                send[slot] = mm_square(state_pair, joins[j][0]) + joins[j][1][
                    piece * rows : (piece + 1) * rows
                ]

                @pl.when(place < places - 1)
                def _():
                    onward(g, j, piece).start()

        for j in range(own):
            slot = g * own + j
            state = jnp.concatenate([recv[slot * PIECES + piece] for piece in range(PIECES)], 0)
            back[slot * SHARE] = state
            for n in range(SHARE - 1):
                step_map = other[slot * SHARE + n]
                state = mm_square(pair(state), step_map[:dim]) + step_map[dim:]
                back[slot * SHARE + n + 1] = state
            for d in range(1, SHARE):
                hand_back(g, j, d).start()
            s_ref[g * group + first + j] = back[slot * SHARE + side]

    @pl.when(turn == parts)
    def _():
        @pl.loop(0, parts)
        def _(g):
            for j in range(own):
                for d in range(1, SHARE):
                    hand_back(g, j, d, True).wait_recv()
                    head = g * group + peer_side(d) * own + j
                    s_ref[head] = mine[head]
                    exchange(g, j, d).wait_send()
                    hand_back(g, j, d).wait_send()

        @pl.when(place < places - 1)
        def _():
            @pl.loop(0, parts)
            def _(g):
                for j in range(own):
                    for piece in range(PIECES):
                        onward(g, j, piece).wait_send()


def out_kernel(pb_ref, s_ref, gate_ref, gain_ref, out_ref, buf):
    group, tok, dim = pb_ref.shape[0], pb_ref.shape[1], pb_ref.shape[2] // 2
    heads = gate_ref.shape[1]
    here = pl.program_id(0) * group
    for g in range(group):
        value = mm_square(pair(pb_ref[g, :, :dim]), s_ref[g].T) + pb_ref[g, :, dim:]
        buf[pl.ds(here + g, tok, stride=heads), :] = value

    @pl.when(pl.program_id(0) == pl.num_programs(0) - 1)
    def _():
        finish(buf, gate_ref, gain_ref, out_ref)


def finish(buf, gate_ref, gain_ref, out_ref):
    tok, heads, dim = gate_ref.shape
    rows = 8 * heads

    @pl.loop(0, tok // 8)
    def _(step):
        value = buf[pl.ds(pl.multiple_of(step * rows, rows), rows), :].reshape(8, heads, dim)
        normed = value / jnp.sqrt(jnp.mean(value * value, -1, keepdims=True) + epsilon)
        gate = jax.nn.silu(gate_ref[pl.ds(step * 8, 8)].astype(F32))
        out_ref[pl.ds(step * 8, 8)] = (normed * gain_ref[...] * gate).astype(out_ref.dtype)


def one_prompt(q, k, v, rate, decay, gate, fq, fk, fv, gain):
    tok, heads, dim = q.shape
    refl = k.shape[1]
    steps = tok * refl
    group = GROUP
    parts = heads // group

    def whole(shape):
        return pl.BlockSpec(shape, lambda i: (0,) * len(shape))

    args = (q, k, v, fq, fk, fv, decay.T, rate.transpose(1, 2, 0))
    half = heads // SHARE
    rim = fq.shape[0] - 1
    dma = pltpu.SemaphoreType.DMA
    pb, states = pl.pallas_call(
        shard_kernel,
        grid=(parts + 1,),
        in_specs=[whole(x.shape) for x in args],
        out_specs=[
            pl.BlockSpec(
                (group, tok, 2 * dim), lambda i: (jnp.minimum(i, parts - 1), 0, 0)
            ),
            whole((heads, dim, dim)),
        ],
        out_shape=[
            jax.ShapeDtypeStruct((heads, tok, 2 * dim), F32),
            jax.ShapeDtypeStruct((heads, dim, dim), F32),
        ],
        scratch_shapes=[
            pltpu.VMEM((tok * heads, dim), F32),
            pltpu.VMEM((steps * heads, dim), F32),
            pltpu.VMEM((steps * heads, dim), F32),
            pltpu.VMEM((steps, heads), F32),
            pltpu.VMEM((steps, heads), F32),
            pltpu.VMEM((tok, heads), F32),
            pltpu.VMEM((rim, heads, dim), BF16),
            pltpu.VMEM((rim, refl, heads, dim), BF16),
            pltpu.VMEM((rim, refl, heads, dim), BF16),
            pltpu.VMEM((heads, 2 * dim, dim), F32),
            pltpu.VMEM((half * SHARE, 2 * dim, dim), F32),
            pltpu.VMEM((half * PIECES, dim // PIECES, dim), F32),
            pltpu.VMEM((half * PIECES, dim // PIECES, dim), F32),
            pltpu.VMEM((heads, dim, dim), F32),
            pltpu.VMEM((heads, dim, dim), F32),
            dma((3,)), dma((3,)), dma((heads,)), dma((heads,)),
            dma((half * PIECES,)), dma((half * PIECES,)), dma((heads,)), dma((heads,)),
        ],
        compiler_params=pltpu.CompilerParams(
            collective_id=0, has_side_effects=True, vmem_limit_bytes=58 * 2**20
        ),
    )(*args)
    return pl.pallas_call(
        out_kernel,
        grid=(parts,),
        in_specs=[
            pl.BlockSpec((group, tok, 2 * dim), lambda i: (i, 0, 0)),
            pl.BlockSpec((group, dim, dim), lambda i: (i, 0, 0)),
            whole((tok, heads, dim)),
            whole((heads, dim)),
        ],
        out_specs=whole((tok, heads, dim)),
        out_shape=jax.ShapeDtypeStruct((tok, heads, dim), BF16),
        scratch_shapes=[pltpu.VMEM((tok * heads, dim), F32)],
        compiler_params=pltpu.CompilerParams(vmem_limit_bytes=58 * 2**20),
    )(pb, states, gate, gain)


def per_device(
    query_raw,
    key_raw,
    value_raw,
    write_rate,
    decay_rate,
    gate_input,
    filter_query,
    filter_key,
    filter_value,
    output_gain,
):
    return jnp.stack(
        [
            one_prompt(
                query_raw[p], key_raw[p], value_raw[p], write_rate[p], decay_rate[p],
                gate_input[p], filter_query, filter_key, filter_value, output_gain,
            )
            for p in range(query_raw.shape[0])
        ]
    )


def solution(mesh):
    return jax.shard_map(
        per_device,
        mesh=mesh,
        in_specs=(
            P(("grp", "prm"), "seq", "hd", None),
            P(("grp", "prm"), "seq", None, "hd", None),
            P(("grp", "prm"), "seq", None, "hd", None),
            P(("grp", "prm"), "seq", None, "hd"),
            P(("grp", "prm"), "seq", "hd"),
            P(("grp", "prm"), "seq", "hd", None),
            P(None, "hd", None),
            P(None, None, "hd", None),
            P(None, None, "hd", None),
            P("hd", None),
        ),
        out_specs=P(("grp", "prm"), "seq", "hd", None),
        check_vma=False,
    )
```

```python
import jax
import jax.numpy as jnp
from jax import lax
from jax.experimental import pallas as pl
from jax.experimental.pallas import tpu as pltpu
from jax.sharding import PartitionSpec as P

HIGH = lax.Precision.HIGHEST
epsilon = 1e-06
CHUNK = 4
GROUP = 4
PIECES = 2
SHARE = 4
F32 = jnp.float32
BF16 = jnp.bfloat16


def split(x):
    hi = x.astype(BF16)
    return hi, (x - hi.astype(F32)).astype(BF16)


def dot(a, b):
    return jnp.dot(a, b, preferred_element_type=F32)


def dot_nt(a, b):
    return lax.dot_general(a, b, (((1,), (1,)), ((), ())), preferred_element_type=F32)


def exact(a, b):
    return jnp.dot(a, b, precision=HIGH, preferred_element_type=F32)


def exact_nt(a, b):
    return lax.dot_general(
        a, b, (((1,), (1,)), ((), ())), precision=HIGH, preferred_element_type=F32
    )


def pair(x):
    return jnp.concatenate(split(x), 1)


def mm_square(left_pair, right):
    rows = pair(right)
    out = dot(left_pair, jnp.concatenate([rows, rows], 0))
    width = right.shape[1]
    return out[:, :width] + out[:, width:]


def mm_wide(left, right):
    left_hi, left_lo = split(left)
    hi, lo = split(right)
    both = jnp.concatenate([left_hi, left_lo], 1)
    return dot(both, jnp.concatenate([hi, hi], 0)) + dot(left_hi, lo)


def mm_deep(left, right):
    left_hi, left_lo = split(left)
    hi, lo = split(right)
    return dot(left_hi, hi) + (dot(left_lo, hi) + dot(left_hi, lo))


def conv_into(x_ref, rim_ref, filter_ref, buf, normalize, edge):
    taps = filter_ref.shape[0]
    rim = taps - 1
    tok = x_ref.shape[0]
    rows = CHUNK * (buf.shape[0] // tok)

    def finish(window, start):
        summed = jnp.zeros((CHUNK,) + window.shape[1:], F32)
        for tap in range(taps):
            summed = summed + filter_ref[tap] * window[tap : tap + CHUNK]
        out = jax.nn.silu(summed)
        if normalize:
            out = out * lax.rsqrt(jnp.sum(out * out, -1, keepdims=True) + epsilon)
        buf[pl.ds(start, rows), :] = out.reshape(rows, out.shape[-1])

    if edge:
        finish(
            jnp.concatenate([rim_ref[...].astype(F32), x_ref[0:CHUNK].astype(F32)], 0), 0
        )
        return

    @pl.loop(1, tok // CHUNK)
    def _(step):
        window = x_ref[pl.ds(step * CHUNK - rim, CHUNK + rim)].astype(F32)
        finish(window, pl.multiple_of(step * rows, rows))


def shard_kernel(
    q_ref, k_ref, v_ref, fq_ref, fk_ref, fv_ref, decay_ref, rate_ref,
    pb_ref, s_ref,
    q_buf, k_buf, v_buf, cum_buf, rate_buf, tok_buf, rim_q, rim_k, rim_v,
    maps, other, recv, send, back, mine,
    rim_send, rim_recv, ex_send, ex_recv, st_send, st_recv, rt_send, rt_recv,
):
    heads, tok, refl, dim = q_ref.shape[1], q_ref.shape[0], k_ref.shape[1], q_ref.shape[2]
    steps = tok * refl
    group = pb_ref.shape[0]
    own = group // SHARE
    parts = heads // group
    rim = rim_q.shape[0]
    turn = pl.program_id(0)

    count = lax.axis_size("seq")
    me = lax.axis_index("seq")
    side = lax.rem(me, SHARE)
    place = lax.div(me, SHARE)
    places = count // SHARE
    base = place * SHARE
    first = side * own

    def remote(src, dst, send_sem, recv_sem, device):
        return pltpu.make_async_remote_copy(
            src_ref=src, dst_ref=dst, send_sem=send_sem, recv_sem=recv_sem,
            device_id={"seq": device}, device_id_type=pl.DeviceIdType.MESH,
        )

    def rim_copies():
        ends = ((q_ref, rim_q), (k_ref, rim_k), (v_ref, rim_v))
        return [
            remote(
                src.at[pl.ds(tok - rim, rim)], dst, rim_send.at[n], rim_recv.at[n],
                lax.rem(me + 1, count),
            )
            for n, (src, dst) in enumerate(ends)
        ]

    def peer_side(d):
        return lax.rem(side + d, SHARE)

    def exchange(g, j, d, arriving=False):
        slot = g * own + j
        peer = peer_side(d)
        source = peer if arriving else side
        return remote(
            maps.at[g * group + peer * own + j], other.at[slot * SHARE + source],
            ex_send.at[slot * SHARE + d], ex_recv.at[slot * SHARE + source], base + peer,
        )

    def onward(g, j, piece):
        slot = (g * own + j) * PIECES + piece
        return remote(
            send.at[slot], recv.at[slot], st_send.at[slot], st_recv.at[slot],
            lax.rem(me + SHARE, count),
        )

    def hand_back(g, j, d, arriving=False):
        slot = g * own + j
        peer = peer_side(d)
        head = g * group + (peer if arriving else side) * own + j
        return remote(
            back.at[slot * SHARE + peer], mine.at[head],
            rt_send.at[slot * SHARE + d], rt_recv.at[head], base + peer,
        )

    @pl.when(turn == 0)
    def _():
        barrier = pltpu.get_barrier_semaphore()

        def signal(device):
            pl.semaphore_signal(
                barrier, inc=1, device_id={"seq": lax.rem(device + count, count)},
                device_id_type=pl.DeviceIdType.MESH,
            )

        for d in range(1, SHARE):
            signal(base + peer_side(d))

        @pl.when(place > 0)
        def _():
            signal(me - SHARE)

            @pl.when(side == 0)
            def _():
                signal(me - 1)

        @pl.when(place < places - 1)
        def _():
            signal(me + SHARE)

            @pl.when(side == SHARE - 1)
            def _():
                signal(me + 1)

        before, after = jnp.minimum(place, 1), jnp.minimum(places - 1 - place, 1)
        peers = SHARE - 1 + before + after
        peers += before * (1 - jnp.minimum(side, 1))
        peers += after * (1 - jnp.minimum(SHARE - 1 - side, 1))
        pl.semaphore_wait(barrier, peers)

        @pl.when(me < count - 1)
        def _():
            for one in rim_copies():
                one.start()

        @pl.when(me == 0)
        def _():
            for one in (rim_q, rim_k, rim_v):
                one[...] = jnp.zeros_like(one)

        @pl.when(place == 0)
        def _():
            recv[...] = jnp.zeros_like(recv)

        def convs(edge):
            conv_into(q_ref, rim_q, fq_ref, q_buf, True, edge)
            conv_into(k_ref, rim_k, fk_ref, k_buf, True, edge)
            conv_into(v_ref, rim_v, fv_ref, v_buf, False, edge)

        convs(False)
        step = lax.broadcasted_iota(jnp.int32, (steps, tok), 0)
        token = lax.broadcasted_iota(jnp.int32, (steps, tok), 1)
        decay = decay_ref[...]
        cum_buf[...] = exact_nt(jnp.where(token * refl <= step, 1.0, 0.0), decay)
        trow = lax.broadcasted_iota(jnp.int32, (tok, tok), 0)
        tcol = lax.broadcasted_iota(jnp.int32, (tok, tok), 1)
        tok_buf[...] = exact_nt(jnp.where(tcol <= trow, 1.0, 0.0), decay)
        rate_buf[...] = sum(
            exact_nt(jnp.where(token * refl + j == step, 1.0, 0.0), rate_ref[j])
            for j in range(refl)
        )

        @pl.when(me > 0)
        def _():
            for one in rim_copies():
                one.wait_recv()

        convs(True)

        @pl.when(me < count - 1)
        def _():
            for one in rim_copies():
                one.wait_send()

    @pl.when(turn < parts)
    def _():
        here = turn * group
        pick = jnp.where(
            lax.broadcasted_iota(jnp.int32, (heads, 128), 0)
            == here + lax.broadcasted_iota(jnp.int32, (heads, 128), 1),
            1.0,
            0.0,
        )
        pick_rows = jnp.where(
            here + lax.broadcasted_iota(jnp.int32, (8, heads), 0)
            == lax.broadcasted_iota(jnp.int32, (8, heads), 1),
            1.0,
            0.0,
        )
        cums = exact(cum_buf[...], pick)
        rates = exact(rate_buf[...], pick)
        toks = exact(tok_buf[...], pick)
        cum_rows = lax.dot_general(
            pick_rows, cum_buf[...], (((1,), (1,)), ((), ())), precision=HIGH,
            preferred_element_type=F32,
        )

        half = steps // 2
        row = lax.broadcasted_iota(jnp.int32, (half, half), 0)
        col = lax.broadcasted_iota(jnp.int32, (half, half), 1)
        qrow = lax.broadcasted_iota(jnp.int32, (tok, steps), 0)
        qcol = lax.broadcasted_iota(jnp.int32, (tok, steps), 1)
        apart = row ^ col
        eye = jnp.where(row == col, 1.0, 0.0)
        dim = q_ref.shape[2]
        drow = lax.broadcasted_iota(jnp.int32, (dim, dim), 0)
        dcol = lax.broadcasted_iota(jnp.int32, (dim, dim), 1)

        work = []
        for g in range(group):
            head = here + g
            K = k_buf[pl.ds(head, steps, stride=heads), :]
            V = v_buf[pl.ds(head, steps, stride=heads), :]
            Q = q_buf[pl.ds(head, tok, stride=heads), :]
            cum = cums[:, g : g + 1]
            rate = rates[:, g : g + 1]
            cum_tok = toks[:, g : g + 1]
            cum_row = cum_rows[g : g + 1, :]
            last = cum_row[:, steps - 1 : steps]
            k_hi, k_lo = split(K)
            q_hi, q_lo = split(Q)
            hi = jnp.concatenate([k_hi, q_hi], 0)
            lo = jnp.concatenate([k_lo, q_lo], 0)
            gram = dot_nt(
                jnp.concatenate([hi, lo], 1), jnp.concatenate([k_hi, k_hi], 1)
            ) + dot_nt(hi, k_lo)

            def lower(r, c):
                ratio = jnp.exp(
                    jnp.minimum(cum_row[:, c * half : (c + 1) * half] - cum[r * half : (r + 1) * half], 0.0)
                )
                block = gram[r * half : (r + 1) * half, c * half : (c + 1) * half]
                value = rate[r * half : (r + 1) * half] * ratio * block
                return jnp.where(row > col, value, 0.0) if r == c else value

            low = [lower(0, 0), lower(1, 1)]
            low_21 = lower(1, 0)
            mixing = jnp.where(
                qrow * refl + (refl - 1) >= qcol,
                gram[steps:] * jnp.exp(jnp.minimum(cum_row - cum_tok, 0.0)),
                0.0,
            )
            right = jnp.concatenate([(rate * jnp.exp(-cum)) * K, rate * V], 1)
            keys_t = K.T * jnp.exp(cum_row - last)
            work.append((low, low_21, mixing, right, keys_t, Q, cum_tok, last))

        inverse = [
            [eye - jnp.where(apart < 2, low, 0.0) for low in item[0]] for item in work
        ]
        size = 2
        while size < half:
            mask = (apart >= size) & (apart < 2 * size)
            lefts = [[pair(x) for x in two] for two in inverse]
            inner = [
                [
                    mm_square(pair(jnp.where(mask, low, 0.0)), x)
                    for low, x in zip(item[0], two)
                ]
                for item, two in zip(work, inverse)
            ]
            inverse = [
                [x - mm_square(l, y) for x, l, y in zip(two, ls, ys)]
                for two, ls, ys in zip(inverse, lefts, inner)
            ]
            size *= 2

        outs = []
        for g, (item, two) in enumerate(zip(work, inverse)):
            low, low_21, mixing, right, keys_t, Q, cum_tok, last = item
            top = mm_wide(two[0], right[:half])
            bottom = mm_wide(two[1], right[half:] - mm_wide(low_21, top))
            solved = jnp.concatenate([top, bottom], 0)
            ab = mm_deep(keys_t, solved)
            maps[here + g, :dim] = jnp.where(drow == dcol, jnp.exp(-last), 0.0) - ab[:, :dim].T
            maps[here + g, dim:] = ab[:, dim:].T
            outs.append((mixing, solved, cum_tok, Q))

        for j in range(own):
            for d in range(1, SHARE):
                exchange(turn, j, d).start()
            other[(turn * own + j) * SHARE + side] = maps[here + first + j]

        for g, (mixing, solved, cum_tok, Q) in enumerate(outs):
            pb = mm_deep(mixing, solved)
            pb_ref[g, :, :dim] = jnp.exp(-cum_tok) * Q - pb[:, :dim]
            pb_ref[g, :, dim:] = pb[:, dim:]

    @pl.when(turn > 0)
    def _():
        g = turn - 1
        joins = []
        for j in range(own):
            for d in range(1, SHARE):
                exchange(g, j, d, True).wait_recv()
            joined = other[(g * own + j) * SHARE]
            for n in range(1, SHARE):
                late = other[(g * own + j) * SHARE + n]
                product = mm_square(pair(joined), late[:dim])
                joined = jnp.concatenate([product[:dim], product[dim:] + late[dim:]], 0)
            joins.append((joined[:dim], joined[dim:]))
        rows = dim // PIECES
        for j in range(own):
            for piece in range(PIECES):

                @pl.when(place > 0)
                def _():
                    onward(g, j, piece).wait_recv()

                slot = (g * own + j) * PIECES + piece
                state_pair = pair(recv[slot])
                send[slot] = mm_square(state_pair, joins[j][0]) + joins[j][1][
                    piece * rows : (piece + 1) * rows
                ]

                @pl.when(place < places - 1)
                def _():
                    onward(g, j, piece).start()

        for j in range(own):
            slot = g * own + j
            state = jnp.concatenate([recv[slot * PIECES + piece] for piece in range(PIECES)], 0)
            back[slot * SHARE] = state
            for n in range(SHARE - 1):
                step_map = other[slot * SHARE + n]
                state = mm_square(pair(state), step_map[:dim]) + step_map[dim:]
                back[slot * SHARE + n + 1] = state
            for d in range(1, SHARE):
                hand_back(g, j, d).start()
            s_ref[g * group + first + j] = back[slot * SHARE + side]

    @pl.when(turn == parts)
    def _():
        @pl.loop(0, parts)
        def _(g):
            for j in range(own):
                for d in range(1, SHARE):
                    hand_back(g, j, d, True).wait_recv()
                    head = g * group + peer_side(d) * own + j
                    s_ref[head] = mine[head]
                    exchange(g, j, d).wait_send()
                    hand_back(g, j, d).wait_send()

        @pl.when(place < places - 1)
        def _():
            @pl.loop(0, parts)
            def _(g):
                for j in range(own):
                    for piece in range(PIECES):
                        onward(g, j, piece).wait_send()


def out_kernel(pb_ref, s_ref, gate_ref, gain_ref, out_ref, buf):
    group, tok, dim = pb_ref.shape[0], pb_ref.shape[1], pb_ref.shape[2] // 2
    heads = gate_ref.shape[1]
    here = pl.program_id(0) * group
    for g in range(group):
        value = mm_square(pair(pb_ref[g, :, :dim]), s_ref[g].T) + pb_ref[g, :, dim:]
        buf[pl.ds(here + g, tok, stride=heads), :] = value

    @pl.when(pl.program_id(0) == pl.num_programs(0) - 1)
    def _():
        finish(buf, gate_ref, gain_ref, out_ref)


def finish(buf, gate_ref, gain_ref, out_ref):
    tok, heads, dim = gate_ref.shape
    rows = 8 * heads

    @pl.loop(0, tok // 8)
    def _(step):
        value = buf[pl.ds(pl.multiple_of(step * rows, rows), rows), :].reshape(8, heads, dim)
        normed = value * lax.rsqrt(jnp.mean(value * value, -1, keepdims=True) + epsilon)
        gate = jax.nn.silu(gate_ref[pl.ds(step * 8, 8)].astype(F32))
        out_ref[pl.ds(step * 8, 8)] = (normed * gain_ref[...] * gate).astype(out_ref.dtype)


def one_prompt(q, k, v, rate, decay, gate, fq, fk, fv, gain):
    tok, heads, dim = q.shape
    refl = k.shape[1]
    steps = tok * refl
    group = GROUP
    parts = heads // group

    def whole(shape):
        return pl.BlockSpec(shape, lambda i: (0,) * len(shape))

    args = (q, k, v, fq, fk, fv, decay.T, rate.transpose(1, 2, 0))
    half = heads // SHARE
    rim = fq.shape[0] - 1
    dma = pltpu.SemaphoreType.DMA
    pb, states = pl.pallas_call(
        shard_kernel,
        grid=(parts + 1,),
        in_specs=[whole(x.shape) for x in args],
        out_specs=[
            pl.BlockSpec(
                (group, tok, 2 * dim), lambda i: (jnp.minimum(i, parts - 1), 0, 0)
            ),
            whole((heads, dim, dim)),
        ],
        out_shape=[
            jax.ShapeDtypeStruct((heads, tok, 2 * dim), F32),
            jax.ShapeDtypeStruct((heads, dim, dim), F32),
        ],
        scratch_shapes=[
            pltpu.VMEM((tok * heads, dim), F32),
            pltpu.VMEM((steps * heads, dim), F32),
            pltpu.VMEM((steps * heads, dim), F32),
            pltpu.VMEM((steps, heads), F32),
            pltpu.VMEM((steps, heads), F32),
            pltpu.VMEM((tok, heads), F32),
            pltpu.VMEM((rim, heads, dim), BF16),
            pltpu.VMEM((rim, refl, heads, dim), BF16),
            pltpu.VMEM((rim, refl, heads, dim), BF16),
            pltpu.VMEM((heads, 2 * dim, dim), F32),
            pltpu.VMEM((half * SHARE, 2 * dim, dim), F32),
            pltpu.VMEM((half * PIECES, dim // PIECES, dim), F32),
            pltpu.VMEM((half * PIECES, dim // PIECES, dim), F32),
            pltpu.VMEM((heads, dim, dim), F32),
            pltpu.VMEM((heads, dim, dim), F32),
            dma((3,)), dma((3,)), dma((heads,)), dma((heads,)),
            dma((half * PIECES,)), dma((half * PIECES,)), dma((heads,)), dma((heads,)),
        ],
        compiler_params=pltpu.CompilerParams(
            collective_id=0, has_side_effects=True, vmem_limit_bytes=58 * 2**20
        ),
    )(*args)
    return pl.pallas_call(
        out_kernel,
        grid=(parts,),
        in_specs=[
            pl.BlockSpec((group, tok, 2 * dim), lambda i: (i, 0, 0)),
            pl.BlockSpec((group, dim, dim), lambda i: (i, 0, 0)),
            whole((tok, heads, dim)),
            whole((heads, dim)),
        ],
        out_specs=whole((tok, heads, dim)),
        out_shape=jax.ShapeDtypeStruct((tok, heads, dim), BF16),
        scratch_shapes=[pltpu.VMEM((tok * heads, dim), F32)],
        compiler_params=pltpu.CompilerParams(vmem_limit_bytes=58 * 2**20),
    )(pb, states, gate, gain)


def per_device(
    query_raw,
    key_raw,
    value_raw,
    write_rate,
    decay_rate,
    gate_input,
    filter_query,
    filter_key,
    filter_value,
    output_gain,
):
    return jnp.stack(
        [
            one_prompt(
                query_raw[p], key_raw[p], value_raw[p], write_rate[p], decay_rate[p],
                gate_input[p], filter_query, filter_key, filter_value, output_gain,
            )
            for p in range(query_raw.shape[0])
        ]
    )


def solution(mesh):
    return jax.shard_map(
        per_device,
        mesh=mesh,
        in_specs=(
            P(("grp", "prm"), "seq", "hd", None),
            P(("grp", "prm"), "seq", None, "hd", None),
            P(("grp", "prm"), "seq", None, "hd", None),
            P(("grp", "prm"), "seq", None, "hd"),
            P(("grp", "prm"), "seq", "hd"),
            P(("grp", "prm"), "seq", "hd", None),
            P(None, "hd", None),
            P(None, None, "hd", None),
            P(None, None, "hd", None),
            P("hd", None),
        ),
        out_specs=P(("grp", "prm"), "seq", "hd", None),
        check_vma=False,
    )
```
